32 devices in a mesh: rows: 4 (over y, core), cols: 8 (over z, x).
Axes of the slice: x: 2, y: 2, z: 4, core: 2. Of those that a mesh axis runs over, the one named last changes fastest.
Arguments:
- band_input: bfloat16 [256, 256, 512], P('rows', 'cols'), may hold values from -1000 to 1000
- column_taps: float32 [21, 512], replicated, may hold values from -1 to 1
- row_taps: float32 [21, 512], replicated, may hold values from -1 to 1
- w_squeeze: bfloat16 [512, 512], replicated, may hold values from -0.25 to 0.25
- bases_init: float32 [512, 64], replicated, may hold values from 0.004 to 0.12
- w_ham: bfloat16 [512, 512], replicated, may hold values from -0.25 to 0.25
- w_align: bfloat16 [512, 512], replicated, may hold values from -0.25 to 0.25
Outputs:
- head_out: bfloat16 [256, 256, 512], P('rows', 'cols')
The draws below stay inside these ranges and needn't reach their ends.
All inputs are finite; a program needn't handle non-finite values.
Results may differ from the reference program's by a relative error of at most 0.0071.
The reference program's roundings to bfloat16 on the way (of `col_filtered`, `mixed_tile`, `feature`, `rebuilt` and `hammed`) count: a program that leaves them out, or rounds other values in their place, can miss the bound.
Values may be sent and summed in bfloat16 or wider, within the bound.
A program may use at most 64 MiB of HBM per device.

```python
import math
import jax
import jax.numpy as jnp
from jax import lax

C = 512
R = 64
KS = 21
STEPS = 3
H = 256
W = 256


def draw_band_input(key, part):
    key_noise, key_phase = jax.random.split(key, 2)
    vertical = (jnp.arange(H, dtype=jnp.float32) / H)[:, None, None]
    horizontal = (jnp.arange(W, dtype=jnp.float32) / W)[None, :, None]
    phases = jax.random.uniform(key_phase, (C,), jnp.float32, 0.0, 6.2831853)[None, None, :]
    smooth = 0.6 * jnp.cos(phases + 6.2831853 * (2.0 * horizontal + vertical))
    jitter = jax.random.truncated_normal(key_noise, -4.0, 4.0, (H, W, C), jnp.float32)
    amplitude = 1.0 + vertical + horizontal
    return (amplitude * (jitter + smooth)).astype(jnp.bfloat16)


def scatter_about(key, shape, width, most, kind=jnp.bfloat16):
    result = jax.random.normal(key, shape, jnp.float32) * width
    return jnp.minimum(jnp.maximum(result, -most), most).astype(kind)


def setup_inputs(seed: int = 0) -> dict:
    streams_of = jax.random.split(jax.random.key(seed), 8)
    return {
        "band_input": draw_band_input(jax.random.fold_in(streams_of[7], 71), 0),
        "column_taps": scatter_about(streams_of[1], (KS, C), 0.2, 1.0, jnp.float32),
        "row_taps": scatter_about(streams_of[2], (KS, C), 0.2, 1.0, jnp.float32),
        "w_squeeze": scatter_about(streams_of[3], (C, C), C ** -0.5, 0.25),
        "bases_init": jnp.clip(jnp.exp(jax.random.uniform(streams_of[4], (C, R), jnp.float32, math.log(0.004), math.log(0.12))), 0.004, 0.12),
        "w_ham": scatter_about(streams_of[5], (C, C), C ** -0.5, 0.25),
        "w_align": scatter_about(streams_of[6], (C, C), C ** -0.5, 0.25),
    }


EPS = 1e-6


def update_coeffs(feature, basis_now, coeffs):
    numerator = jnp.dot(feature, basis_now.astype(jnp.bfloat16), preferred_element_type=jnp.float32)
    gram_local = jnp.dot(basis_now.T, basis_now, precision=lax.Precision.HIGHEST)
    denominator = jnp.dot(coeffs, gram_local, precision=lax.Precision.HIGHEST)
    return coeffs * numerator / (denominator + EPS)


def reference(band_input, column_taps, row_taps, w_squeeze, bases_init, w_ham, w_align):
    margin = KS // 2
    padded = jnp.pad(band_input, ((0, 0), (margin, margin), (0, 0)))
    summed = jnp.zeros((H, W, C), jnp.float32)
    for offset in range(KS):
        summed = summed + column_taps[offset] * padded[:, offset:offset + W, :].astype(jnp.float32)
    col_filtered = summed.astype(jnp.bfloat16)
    padded = jnp.pad(col_filtered, ((margin, margin), (0, 0), (0, 0)))
    strip_sum = jnp.zeros((H, W, C), jnp.float32)
    for offset in range(KS):
        strip_sum = strip_sum + row_taps[offset] * padded[offset:offset + H].astype(jnp.float32)
    mixed_tile = (band_input.astype(jnp.float32) + strip_sum).astype(jnp.bfloat16).reshape(H * W, C)
    feature = jax.nn.relu(jnp.dot(mixed_tile, w_squeeze, preferred_element_type=jnp.float32)).astype(jnp.bfloat16)
    basis_now = bases_init
    scores = jnp.dot(feature, basis_now.astype(jnp.bfloat16), preferred_element_type=jnp.float32)
    coeffs = jax.nn.softmax(scores, axis=-1)
    for iteration in range(STEPS):
        coeffs = update_coeffs(feature, basis_now, coeffs)
        numerator = jnp.dot(feature.T, coeffs.astype(jnp.bfloat16), preferred_element_type=jnp.float32)
        gram_sum = jnp.dot(coeffs.T, coeffs, precision=lax.Precision.HIGHEST)
        basis_now = basis_now * numerator / (jnp.dot(basis_now, gram_sum, precision=lax.Precision.HIGHEST) + EPS)
    coeffs = update_coeffs(feature, basis_now, coeffs)
    rebuilt = jnp.dot(coeffs.astype(jnp.bfloat16), basis_now.astype(jnp.bfloat16).T, preferred_element_type=jnp.float32).astype(jnp.bfloat16)
    ham_term = jnp.dot(rebuilt, w_ham, preferred_element_type=jnp.float32)
    hammed = jax.nn.relu(feature.astype(jnp.float32) + ham_term).astype(jnp.bfloat16)
    head_out = jnp.dot(hammed, w_align, preferred_element_type=jnp.float32).astype(jnp.bfloat16)
    return head_out.reshape(H, W, C)
```

```python
import functools

import jax
import jax.numpy as jnp
from jax import lax
from jax.experimental import pallas as pl
from jax.experimental.pallas import tpu as pltpu
from jax.sharding import PartitionSpec as P

STEPS = 3


EPS = 1e-06

MESH = pl.DeviceIdType.MESH
HIGHEST = lax.Precision.HIGHEST
NT = (((1,), (1,)), ((), ()))


def padded(x, sides, width):
    for axis, dim in sides:
        count, length = (lax.axis_size(axis), x.shape[dim])
        up = [(i, (i + 1) % count) for i in range(count - 1)]
        down = [(j, i) for i, j in up]
        last = lax.slice_in_dim(x, length - width, length, axis=dim)
        initial = lax.slice_in_dim(x, 0, width, axis=dim)
        before = lax.ppermute(last, axis, up)
        after = lax.ppermute(initial, axis, down)
        x = jnp.concatenate([before, x, after], axis=dim)
    return x


def filter_columns(widened, column_taps, extent):
    summed = jnp.zeros((widened.shape[0], extent, widened.shape[2]), jnp.float32)
    for offset in range(column_taps.shape[0]):
        summed = summed + column_taps[offset] * widened[:, offset : offset + extent, :].astype(
            jnp.float32
        )
    return summed


def filter_rows(extended, row_taps, extent):
    summed = jnp.zeros((extent, extended.shape[1], extended.shape[2]), jnp.float32)
    for offset in range(row_taps.shape[0]):
        summed = summed + row_taps[offset] * extended[offset : offset + extent].astype(jnp.float32)
    return summed


def dot32(a, b):
    return jnp.dot(a, b, preferred_element_type=jnp.float32)


def factor_kernel(
    grid_shape, mixed, w_squeeze, bases, w_ham, w_align, out,
    feature, coeffs, basis_now, part, arrived, line_out, line_in, gathered,
    a_send, a_recv, b_send, b_recv, c_send, c_recv,
):
    n_rows, n_cols, pair, piece = grid_shape
    group, line = n_rows * pair, n_cols // pair
    pixels, channels = mixed.shape
    rank = bases.shape[0]
    depth = rank // group
    blocks = pixels // piece

    row, col = lax.axis_index("rows"), lax.axis_index("cols")
    cell, along = lax.rem(col, pair), lax.div(col, pair)
    member = row * pair + cell

    def in_group(step):
        other = lax.rem(member + step, group)
        return other, (lax.div(other, pair), along * pair + lax.rem(other, pair))

    def in_line(step):
        return (row, lax.rem(along + step, line) * pair + cell)

    barrier = pltpu.get_barrier_semaphore()
    for step in range(1, group):
        pl.semaphore_signal(barrier, inc=1, device_id=in_group(step)[1], device_id_type=MESH)
    for step in range(1, line):
        pl.semaphore_signal(barrier, inc=1, device_id=in_line(step), device_id_type=MESH)

    def copy_a(it, step):
        other, device = in_group(step)
        return pltpu.make_async_remote_copy(
            src_ref=part.at[it, other], dst_ref=arrived.at[it, step],
            send_sem=a_send.at[it, step], recv_sem=a_recv.at[it, step],
            device_id=device, device_id_type=MESH,
        )

    def copy_b(it, step):
        return pltpu.make_async_remote_copy(
            src_ref=line_out.at[it], dst_ref=line_in.at[it, step],
            send_sem=b_send.at[it, step], recv_sem=b_recv.at[it, step],
            device_id=in_line(step), device_id_type=MESH,
        )

    def copy_c(it, step, slot):
        return pltpu.make_async_remote_copy(
            src_ref=gathered.at[it, slot], dst_ref=gathered.at[it, slot],
            send_sem=c_send.at[it, step], recv_sem=c_recv.at[it, step],
            device_id=in_group(step)[1], device_id_type=MESH,
        )

    def reduce_all(it, numerator, gram):
        both = jnp.concatenate([numerator, gram, jnp.zeros_like(gram)], axis=1)
        for index in range(group):
            part[it, index] = both[index * depth : (index + 1) * depth]
        if it == 0:
            pl.semaphore_wait(barrier, group - 1 + line - 1)
        for step in range(1, group):
            copy_a(it, step).start()
        total = part[it, member]
        for step in range(1, group):
            copy_a(it, step).wait_recv()
            total = total + arrived[it, step]
        if line > 1:
            line_out[it] = total
            for step in range(1, line):
                copy_b(it, step).start()
            for step in range(1, line):
                copy_b(it, step).wait_recv()
                total = total + line_in[it, step]
        gathered[it, member] = total
        for step in range(1, group):
            copy_c(it, step, member).start()
        for step in range(1, group):
            copy_c(it, step, lax.rem(member + group - step, group)).wait_recv()
        whole = jnp.concatenate([gathered[it, index] for index in range(group)], axis=0)
        return whole[:, :channels], whole[:, channels : channels + rank]

    def sums(it):
        basis = basis_now[...]
        basis_low = basis.astype(jnp.bfloat16)
        gram_local = lax.dot_general(
            basis, basis, NT, precision=HIGHEST, preferred_element_type=jnp.float32
        )

        def body(index, carry):
            numerator, gram = carry
            span = pl.ds(pl.multiple_of(index * piece, piece), piece)
            if it == 0:
                f = jnp.maximum(dot32(mixed[span, :], w_squeeze[...]), 0.0).astype(jnp.bfloat16)
                feature[span, :] = f
            else:
                f = feature[span, :]
            top = lax.dot_general(basis_low, f, NT, preferred_element_type=jnp.float32)
            if it == 0:
                weight = jnp.exp(top - jnp.max(top, axis=0, keepdims=True))
                now = weight / jnp.sum(weight, axis=0, keepdims=True)
            else:
                now = coeffs[index]
            below = jnp.dot(gram_local, now, precision=HIGHEST, preferred_element_type=jnp.float32)
            now = now * top / (below + EPS)
            if it < STEPS:
                coeffs[index] = now
                numerator = numerator + dot32(now.astype(jnp.bfloat16), f)
                gram = gram + lax.dot_general(
                    now, now, NT, precision=HIGHEST, preferred_element_type=jnp.float32
                )
                return numerator, gram
            rebuilt = lax.dot_general(
                now.astype(jnp.bfloat16), basis_low, (((0,), (0,)), ((), ())),
                preferred_element_type=jnp.float32,
            ).astype(jnp.bfloat16)
            hammed = jnp.maximum(f.astype(jnp.float32) + dot32(rebuilt, w_ham[...]), 0.0)
            out[span, :] = dot32(hammed.astype(jnp.bfloat16), w_align[...]).astype(jnp.bfloat16)
            return carry

        start = (jnp.zeros((rank, channels), jnp.float32), jnp.zeros((rank, rank), jnp.float32))
        if it < STEPS:
            return lax.fori_loop(0, blocks, body, start)
        lax.fori_loop(0, blocks, lambda i, c: (body(i, start), c)[1], 0)

    basis_now[...] = bases[...]
    for it in range(STEPS):
        numerator, gram = reduce_all(it, *sums(it))
        basis = basis_now[...]
        below = jnp.dot(gram, basis, precision=HIGHEST, preferred_element_type=jnp.float32)
        basis_now[...] = basis * numerator / (below + EPS)
    sums(STEPS)
    for it in range(STEPS):
        for step in range(1, group):
            copy_a(it, step).wait_send()
            copy_c(it, step, member).wait_send()
        for step in range(1, line):
            copy_b(it, step).wait_send()


def factor(mixed, w_squeeze, bases_init, w_ham, w_align):
    n_rows, n_cols = lax.axis_size("rows"), lax.axis_size("cols")
    pair = 2 if n_cols % 2 == 0 else 1
    group, line = n_rows * pair, n_cols // pair
    pixels, channels = mixed.shape
    rank = bases_init.shape[1]
    depth, width = rank // group, channels + 2 * rank
    piece = 512 if pixels % 512 == 0 else pixels
    dma = pltpu.SemaphoreType.DMA
    vmem = pl.BlockSpec(memory_space=pltpu.VMEM)
    return pl.pallas_call(
        functools.partial(factor_kernel, (n_rows, n_cols, pair, piece)),
        out_shape=jax.ShapeDtypeStruct((pixels, channels), jnp.bfloat16),
        in_specs=[vmem] * 5,
        out_specs=vmem,
        scratch_shapes=[
            pltpu.VMEM((pixels, channels), jnp.bfloat16),
            pltpu.VMEM((pixels // piece, rank, piece), jnp.float32),
            pltpu.VMEM((rank, channels), jnp.float32),
            pltpu.VMEM((STEPS, group, depth, width), jnp.float32),
            pltpu.VMEM((STEPS, group, depth, width), jnp.float32),
            pltpu.VMEM((STEPS, depth, width), jnp.float32),
            pltpu.VMEM((STEPS, line, depth, width), jnp.float32),
            pltpu.VMEM((STEPS, group, depth, width), jnp.float32),
            dma((STEPS, group)), dma((STEPS, group)),
            dma((STEPS, line)), dma((STEPS, line)),
            dma((STEPS, group)), dma((STEPS, group)),
        ],
        compiler_params=pltpu.CompilerParams(
            collective_id=0, has_side_effects=True, vmem_limit_bytes=40 * 2**20
        ),
        cost_estimate=pl.CostEstimate(
            flops=6 * pixels * channels * channels, bytes_accessed=8 * pixels * channels,
            transcendentals=0,
        ),
    )(mixed, w_squeeze, bases_init.T, w_ham, w_align)


def on_device(band_input, column_taps, row_taps, w_squeeze, bases_init, w_ham, w_align):
    tile_rows, tile_cols, channels = band_input.shape
    margin = column_taps.shape[0] // 2
    widened = padded(band_input, (("cols", 1),), margin)
    col_filtered = filter_columns(widened, column_taps, tile_cols).astype(jnp.bfloat16)
    extended = padded(col_filtered, (("rows", 0),), margin)
    strip_sum = filter_rows(extended, row_taps, tile_rows)
    mixed_tile = (
        (band_input.astype(jnp.float32) + strip_sum)
        .astype(jnp.bfloat16)
        .reshape(tile_rows * tile_cols, channels)
    )
    head_out = factor(mixed_tile, w_squeeze, bases_init, w_ham, w_align)
    return head_out.reshape(tile_rows, tile_cols, channels)


def solution(mesh):
    in_specs = (P("rows", "cols", None), P(), P(), P(), P(), P(), P())
    out_specs = P("rows", "cols", None)
    return jax.shard_map(
        on_device, mesh=mesh, in_specs=in_specs, out_specs=out_specs, check_vma=False
    )
```

```python
import functools

import jax
import jax.numpy as jnp
from jax import lax
from jax.experimental import pallas as pl
from jax.experimental.pallas import tpu as pltpu
from jax.sharding import PartitionSpec as P

STEPS = 3


EPS = 1e-06

MESH = pl.DeviceIdType.MESH
HIGHEST = lax.Precision.HIGHEST
NT = (((1,), (1,)), ((), ()))


def dot32(a, b):
    return jnp.dot(a, b, preferred_element_type=jnp.float32)


def strip(load, taps, count):
    results = [None] * count
    for index in range(count + len(taps) - 1):
        x = load(index).astype(jnp.float32)
        for target in range(max(0, index - len(taps) + 1), min(count, index + 1)):
            term = taps[index - target] * x
            results[target] = term if results[target] is None else results[target] + term
    return results


def filter_strips(
    counts, row, col, greet, band, column_taps, row_taps, mixed, wide, tall,
    w_send, w_recv, t_send, t_recv,
):
    n_rows, n_cols = counts
    tile_rows, tile_cols, channels = band.shape
    taps = column_taps.shape[0]
    margin = taps // 2
    lanes = wide.shape[3]
    blocks = channels // lanes
    has = (
        (col > 0, col < n_cols - 1),
        (row > 0, row < n_rows - 1),
    )

    def edge_copy(axis, block, side):
        buffer, length = ((wide, tile_cols), (tall, tile_rows))[axis]
        send, recv = ((w_send, w_recv), (t_send, t_recv))[axis]
        start = margin if side == 0 else length
        target = margin + length if side == 0 else 0
        step = -1 if side == 0 else 1
        device = (row, col + step) if axis == 0 else (row + step, col)
        return pltpu.make_async_remote_copy(
            src_ref=buffer.at[block, pl.ds(start, margin)],
            dst_ref=buffer.at[block, pl.ds(target, margin)],
            send_sem=send.at[block, side], recv_sem=recv.at[block, side],
            device_id=device, device_id_type=MESH,
        )

    def start(axis, block):
        for side in range(2):
            @pl.when(has[axis][side])
            def _():
                edge_copy(axis, block, side).start()

    def wait_send(axis, block):
        for side in range(2):
            @pl.when(has[axis][side])
            def _():
                edge_copy(axis, block, side).wait_send()

    def wait_recv(axis, block):
        for side in range(2):
            @pl.when(has[axis][1 - side])
            def _():
                edge_copy(axis, block, side).wait_recv()

    def clear(axis):
        buffer, length = ((wide, tile_cols), (tall, tile_rows))[axis]
        for side, first in ((0, 0), (1, margin + length)):
            @pl.when(jnp.logical_not(has[axis][side]))
            def _():
                @pl.loop(0, blocks)
                def _(block):
                    buffer[block, first : first + margin] = jnp.zeros(
                        (margin,) + buffer.shape[2:], buffer.dtype
                    )

    def turn(block):
        span = slice(block * lanes, (block + 1) * lanes)

        @pl.loop(0, tile_rows // 16)
        def _(index):
            rows = pl.ds(pl.multiple_of(index * 16, 16), 16)
            x = band[rows, :, span].astype(jnp.float32)
            wide[block, margin : margin + tile_cols, rows, :] = jnp.swapaxes(x, 0, 1).astype(
                jnp.bfloat16
            )

    def across(block):
        span = slice(block * lanes, (block + 1) * lanes)
        halves = tile_cols // 16

        @pl.loop(0, (tile_rows // 16) * halves)
        def _(index):
            h = lax.div(index, halves) * 16
            w = lax.rem(index, halves) * 16
            rows = pl.ds(pl.multiple_of(h, 16), 16)
            factors = [column_taps[k : k + 1, span] for k in range(taps)]
            found = []
            for part in range(2):
                found += strip(
                    lambda i: wide[block, w + part * 8 + i, rows, :], factors, 8
                )
            x = jnp.swapaxes(jnp.stack(found, axis=0), 0, 1).astype(jnp.bfloat16)
            tall[block, pl.ds(margin + h, 16), pl.ds(pl.multiple_of(w, 16), 16), :] = x

    def down(block):
        span = slice(block * lanes, (block + 1) * lanes)
        halves = tile_cols // 16

        @pl.loop(0, (tile_rows // 8) * halves)
        def _(index):
            h = lax.div(index, halves) * 8
            w = pl.multiple_of(lax.rem(index, halves) * 16, 16)
            factors = [row_taps[k : k + 1, span] for k in range(taps)]
            found = strip(lambda i: tall[block, h + i, pl.ds(w, 16), :], factors, 8)
            for i in range(8):
                x = band[h + i, pl.ds(w, 16), span].astype(jnp.float32) + found[i]
                place = pl.ds(pl.multiple_of((h + i) * tile_cols + w, 16), 16)
                mixed[place, span] = x.astype(jnp.bfloat16)

    turn(0)
    greet()
    start(0, 0)
    ahead = min(2, blocks)
    for block in range(1, blocks):
        turn(block)
        if block < ahead:
            start(0, block)
    clear(0)
    clear(1)
    for block in range(blocks):
        if block + ahead < blocks:
            wait_send(0, block)
            start(0, block + ahead)
        wait_recv(0, block)
        across(block)
        start(1, block)
        if block > 0:
            wait_recv(1, block - 1)
            down(block - 1)
    wait_recv(1, blocks - 1)
    down(blocks - 1)
    for block in range(blocks):
        if block + ahead >= blocks:
            wait_send(0, block)
        wait_send(1, block)


def factor_kernel(
    grid_shape, band, column_taps, row_taps, w_squeeze, bases, w_ham, w_align, out,
    wide, tall, mixed, feature, coeffs, basis_now, part, arrived, line_out, line_in, gathered,
    w_send, w_recv, t_send, t_recv, a_send, a_recv, b_send, b_recv, c_send, c_recv,
):
    n_rows, n_cols, pair, piece = grid_shape
    group, line = n_rows * pair, n_cols // pair
    pixels, channels = mixed.shape
    rank = bases.shape[0]
    depth = rank // group
    blocks = pixels // piece

    row, col = lax.axis_index("rows"), lax.axis_index("cols")
    cell, along = lax.rem(col, pair), lax.div(col, pair)
    member = row * pair + cell

    def in_group(step):
        other = lax.rem(member + step, group)
        return other, (lax.div(other, pair), along * pair + lax.rem(other, pair))

    def in_line(step):
        return (row, lax.rem(along + step, line) * pair + cell)

    barrier = pltpu.get_barrier_semaphore()
    for step in range(1, group):
        pl.semaphore_signal(barrier, inc=1, device_id=in_group(step)[1], device_id_type=MESH)
    for step in range(1, line):
        pl.semaphore_signal(barrier, inc=1, device_id=in_line(step), device_id_type=MESH)
    greeted = group - 1 + line - 1
    if pair == 2:
        outer = jnp.where(cell == 0, col - 1, col + 1)
        has_outer = jnp.logical_and(outer >= 0, outer < n_cols)

        @pl.when(has_outer)
        def _():
            pl.semaphore_signal(barrier, inc=1, device_id=(row, outer), device_id_type=MESH)

        greeted = greeted + has_outer.astype(jnp.int32)

    filter_strips(
        (n_rows, n_cols), row, col, lambda: pl.semaphore_wait(barrier, greeted),
        band, column_taps, row_taps, mixed, wide, tall, w_send, w_recv, t_send, t_recv,
    )

    def copy_a(it, step):
        other, device = in_group(step)
        return pltpu.make_async_remote_copy(
            src_ref=part.at[it, other], dst_ref=arrived.at[it, step],
            send_sem=a_send.at[it, step], recv_sem=a_recv.at[it, step],
            device_id=device, device_id_type=MESH,
        )

    def copy_b(it, step):
        return pltpu.make_async_remote_copy(
            src_ref=line_out.at[it], dst_ref=line_in.at[it, step],
            send_sem=b_send.at[it, step], recv_sem=b_recv.at[it, step],
            device_id=in_line(step), device_id_type=MESH,
        )

    def copy_c(it, step, slot):
        return pltpu.make_async_remote_copy(
            src_ref=gathered.at[it, slot], dst_ref=gathered.at[it, slot],
            send_sem=c_send.at[it, step], recv_sem=c_recv.at[it, step],
            device_id=in_group(step)[1], device_id_type=MESH,
        )

    def reduce_all(it, numerator, gram):
        both = jnp.concatenate([numerator, gram, jnp.zeros_like(gram)], axis=1)
        for index in range(group):
            part[it, index] = both[index * depth : (index + 1) * depth]
        for step in range(1, group):
            copy_a(it, step).start()
        total = part[it, member]
        for step in range(1, group):
            copy_a(it, step).wait_recv()
            total = total + arrived[it, step]
        if line > 1:
            line_out[it] = total
            for step in range(1, line):
                copy_b(it, step).start()
            for step in range(1, line):
                copy_b(it, step).wait_recv()
                total = total + line_in[it, step]
        gathered[it, member] = total
        for step in range(1, group):
            copy_c(it, step, member).start()
        for step in range(1, group):
            copy_c(it, step, lax.rem(member + group - step, group)).wait_recv()
        whole = jnp.concatenate([gathered[it, index] for index in range(group)], axis=0)
        return whole[:, :channels], whole[:, channels : channels + rank]

    def sums(it):
        basis = basis_now[...]
        basis_low = basis.astype(jnp.bfloat16)
        gram_local = lax.dot_general(
            basis, basis, NT, precision=HIGHEST, preferred_element_type=jnp.float32
        )

        def body(index, carry):
            numerator, gram = carry
            span = pl.ds(pl.multiple_of(index * piece, piece), piece)
            if it == 0:
                f = jnp.maximum(dot32(mixed[span, :], w_squeeze[...]), 0.0).astype(jnp.bfloat16)
                feature[span, :] = f
            else:
                f = feature[span, :]
            top = lax.dot_general(basis_low, f, NT, preferred_element_type=jnp.float32)
            if it == 0:
                weight = jnp.exp(top - jnp.max(top, axis=0, keepdims=True))
                now = weight / jnp.sum(weight, axis=0, keepdims=True)
            else:
                now = coeffs[index]
            below = jnp.dot(gram_local, now, precision=HIGHEST, preferred_element_type=jnp.float32)
            now = now * top / (below + EPS)
            if it < STEPS:
                coeffs[index] = now
                numerator = numerator + dot32(now.astype(jnp.bfloat16), f)
                gram = gram + lax.dot_general(
                    now, now, NT, precision=HIGHEST, preferred_element_type=jnp.float32
                )
                return numerator, gram
            rebuilt = lax.dot_general(
                now.astype(jnp.bfloat16), basis_low, (((0,), (0,)), ((), ())),
                preferred_element_type=jnp.float32,
            ).astype(jnp.bfloat16)
            hammed = jnp.maximum(f.astype(jnp.float32) + dot32(rebuilt, w_ham[...]), 0.0)
            out[span, :] = dot32(hammed.astype(jnp.bfloat16), w_align[...]).astype(jnp.bfloat16)
            return carry

        start = (jnp.zeros((rank, channels), jnp.float32), jnp.zeros((rank, rank), jnp.float32))
        if it < STEPS:
            return lax.fori_loop(0, blocks, body, start)
        lax.fori_loop(0, blocks, lambda i, c: (body(i, start), c)[1], 0)

    basis_now[...] = bases[...]
    for it in range(STEPS):
        numerator, gram = reduce_all(it, *sums(it))
        basis = basis_now[...]
        below = jnp.dot(gram, basis, precision=HIGHEST, preferred_element_type=jnp.float32)
        basis_now[...] = basis * numerator / (below + EPS)
    sums(STEPS)
    for it in range(STEPS):
        for step in range(1, group):
            copy_a(it, step).wait_send()
            copy_c(it, step, member).wait_send()
        for step in range(1, line):
            copy_b(it, step).wait_send()


def on_device(band_input, column_taps, row_taps, w_squeeze, bases_init, w_ham, w_align):
    n_rows, n_cols = lax.axis_size("rows"), lax.axis_size("cols")
    pair = 2 if n_cols % 2 == 0 else 1
    group, line = n_rows * pair, n_cols // pair
    tile_rows, tile_cols, channels = band_input.shape
    pixels = tile_rows * tile_cols
    margin = column_taps.shape[0] // 2
    rank = bases_init.shape[1]
    depth, width = rank // group, channels + 2 * rank
    piece = 512 if pixels % 512 == 0 else pixels
    lanes = 128
    blocks = channels // lanes
    dma = pltpu.SemaphoreType.DMA
    vmem = pl.BlockSpec(memory_space=pltpu.VMEM)
    head_out = pl.pallas_call(
        functools.partial(factor_kernel, (n_rows, n_cols, pair, piece)),
        out_shape=jax.ShapeDtypeStruct((pixels, channels), jnp.bfloat16),
        in_specs=[vmem] * 7,
        out_specs=vmem,
        scratch_shapes=[
            pltpu.VMEM((blocks, tile_cols + 2 * margin, tile_rows, lanes), jnp.bfloat16),
            pltpu.VMEM((blocks, tile_rows + 2 * margin, tile_cols, lanes), jnp.bfloat16),
            pltpu.VMEM((pixels, channels), jnp.bfloat16),
            pltpu.VMEM((pixels, channels), jnp.bfloat16),
            pltpu.VMEM((pixels // piece, rank, piece), jnp.float32),
            pltpu.VMEM((rank, channels), jnp.float32),
            pltpu.VMEM((STEPS, group, depth, width), jnp.float32),
            pltpu.VMEM((STEPS, group, depth, width), jnp.float32),
            pltpu.VMEM((STEPS, depth, width), jnp.float32),
            pltpu.VMEM((STEPS, line, depth, width), jnp.float32),
            pltpu.VMEM((STEPS, group, depth, width), jnp.float32),
            dma((blocks, 2)), dma((blocks, 2)),
            dma((blocks, 2)), dma((blocks, 2)),
            dma((STEPS, group)), dma((STEPS, group)),
            dma((STEPS, line)), dma((STEPS, line)),
            dma((STEPS, group)), dma((STEPS, group)),
        ],
        compiler_params=pltpu.CompilerParams(
            collective_id=0, has_side_effects=True, vmem_limit_bytes=48 * 2**20
        ),
        cost_estimate=pl.CostEstimate(
            flops=6 * pixels * channels * channels, bytes_accessed=8 * pixels * channels,
            transcendentals=0,
        ),
    )(band_input, column_taps, row_taps, w_squeeze, bases_init.T, w_ham, w_align)
    return head_out.reshape(tile_rows, tile_cols, channels)


def solution(mesh):
    in_specs = (P("rows", "cols", None), P(), P(), P(), P(), P(), P())
    out_specs = P("rows", "cols", None)
    return jax.shard_map(
        on_device, mesh=mesh, in_specs=in_specs, out_specs=out_specs, check_vma=False
    )
```

```python
import functools

import jax
import jax.numpy as jnp
from jax import lax
from jax.experimental import pallas as pl
from jax.experimental.pallas import tpu as pltpu
from jax.sharding import PartitionSpec as P

STEPS = 3


EPS = 1e-06

MESH = pl.DeviceIdType.MESH
NT = (((1,), (1,)), ((), ()))


def dot32(a, b):
    return jnp.dot(a, b, preferred_element_type=jnp.float32)


def strip(load, taps, count):
    results = [None] * count
    for index in range(count + len(taps) - 1):
        x = load(index).astype(jnp.float32)
        for target in range(max(0, index - len(taps) + 1), min(count, index + 1)):
            term = taps[index - target] * x
            results[target] = term if results[target] is None else results[target] + term
    return results


def filter_strips(
    counts, row, col, greet, load_band, loads, band, column_taps, row_taps, mixed, wide, tall,
    w_send, w_recv, t_send, t_recv,
):
    n_rows, n_cols = counts
    tile_rows, tile_cols, channels = band.shape
    taps = column_taps.shape[0]
    margin = taps // 2
    lanes = wide.shape[3]
    blocks = channels // lanes
    has = (
        (col > 0, col < n_cols - 1),
        (row > 0, row < n_rows - 1),
    )

    def edge_copy(axis, block, side):
        buffer, length = ((wide, tile_cols), (tall, tile_rows))[axis]
        send, recv = ((w_send, w_recv), (t_send, t_recv))[axis]
        start = margin if side == 0 else length
        target = margin + length if side == 0 else 0
        step = -1 if side == 0 else 1
        device = (row, col + step) if axis == 0 else (row + step, col)
        return pltpu.make_async_remote_copy(
            src_ref=buffer.at[block, pl.ds(start, margin)],
            dst_ref=buffer.at[block, pl.ds(target, margin)],
            send_sem=send.at[block, side], recv_sem=recv.at[block, side],
            device_id=device, device_id_type=MESH,
        )

    def start(axis, block):
        for side in range(2):
            @pl.when(has[axis][side])
            def _():
                edge_copy(axis, block, side).start()

    def wait_send(axis, block):
        for side in range(2):
            @pl.when(has[axis][side])
            def _():
                edge_copy(axis, block, side).wait_send()

    def wait_recv(axis, block):
        for side in range(2):
            @pl.when(has[axis][1 - side])
            def _():
                edge_copy(axis, block, side).wait_recv()

    def clear(axis):
        buffer, length = ((wide, tile_cols), (tall, tile_rows))[axis]
        for side, first in ((0, 0), (1, margin + length)):
            @pl.when(jnp.logical_not(has[axis][side]))
            def _():
                @pl.loop(0, blocks)
                def _(block):
                    buffer[block, first : first + margin] = jnp.zeros(
                        (margin,) + buffer.shape[2:], buffer.dtype
                    )

    def turn(block):
        span = slice(block * lanes, (block + 1) * lanes)

        @pl.loop(0, tile_rows // 16)
        def _(index):
            rows = pl.ds(pl.multiple_of(index * 16, 16), 16)
            x = band[rows, :, span].astype(jnp.float32)
            wide[block, margin : margin + tile_cols, rows, :] = jnp.swapaxes(x, 0, 1).astype(
                jnp.bfloat16
            )

    def across(block):
        span = slice(block * lanes, (block + 1) * lanes)
        halves = tile_cols // 16

        @pl.loop(0, (tile_rows // 16) * halves)
        def _(index):
            h = lax.div(index, halves) * 16
            w = lax.rem(index, halves) * 16
            rows = pl.ds(pl.multiple_of(h, 16), 16)
            factors = [column_taps[k : k + 1, span] for k in range(taps)]
            found = []
            for part in range(2):
                found += strip(
                    lambda i: wide[block, w + part * 8 + i, rows, :], factors, 8
                )
            x = jnp.swapaxes(jnp.stack(found, axis=0), 0, 1).astype(jnp.bfloat16)
            tall[block, pl.ds(margin + h, 16), pl.ds(pl.multiple_of(w, 16), 16), :] = x

    def down(block, first, last):
        span = slice(block * lanes, (block + 1) * lanes)
        halves = tile_cols // 16

        @pl.loop(first * halves, last * halves)
        def _(index):
            h = lax.div(index, halves) * 8
            w = pl.multiple_of(lax.rem(index, halves) * 16, 16)
            factors = [row_taps[k : k + 1, span] for k in range(taps)]
            found = strip(lambda i: tall[block, h + i, pl.ds(w, 16), :], factors, 8)
            for i in range(8):
                x = band[h + i, pl.ds(w, 16), span].astype(jnp.float32) + found[i]
                place = pl.ds(pl.multiple_of((h + i) * tile_cols + w, 16), 16)
                mixed[place, span] = x.astype(jnp.bfloat16)

    load_band(0).wait()
    turn(0)
    greet()
    start(0, 0)
    ahead = min(2, blocks)
    for block in range(1, blocks):
        load_band(block).wait()
        turn(block)
        if block < ahead:
            start(0, block)
    clear(0)
    clear(1)
    for load in loads:
        load.wait()
    strips = tile_rows // 8
    edge = -(-margin // 8)
    for block in range(blocks):
        if block + ahead < blocks:
            wait_send(0, block)
            start(0, block + ahead)
        wait_recv(0, block)
        across(block)
        start(1, block)
        down(block, edge, strips - edge)
        wait_recv(1, block)
        down(block, 0, edge)
        down(block, strips - edge, strips)
    for block in range(blocks):
        if block + ahead >= blocks:
            wait_send(0, block)
        wait_send(1, block)


def split(x):
    high = x.astype(jnp.bfloat16)
    return high, (x - high.astype(jnp.float32)).astype(jnp.bfloat16)


def product(a, b):
    a_high, a_low = split(a)
    b_high, b_low = split(b)
    return dot32(
        jnp.concatenate([a_high, a_low, a_high], axis=1),
        jnp.concatenate([b_high, b_high, b_low], axis=0),
    )


def gram_of(stacked):
    n = stacked.shape[0] // 2
    both = lax.dot_general(stacked, stacked, NT, preferred_element_type=jnp.float32)
    return both[:n, :n] + (both[:n, n:] + both[n:, :n])


def factor_kernel(
    grid_shape, *refs,
):
    sources, out = refs[:7], refs[7]
    band, column_taps, row_taps, w_squeeze, basis_now, w_ham, w_align = refs[8:15]
    (
    wide, tall, mixed, feature, coeffs, halves, part, arrived, line_out, line_in, gathered,
    w_send, w_recv, t_send, t_recv, a_send, a_recv, b_send, b_recv, c_send, c_recv,
    load_sem, band_sem, out_sem,
    ) = refs[15:]
    n_rows, n_cols, pair, piece = grid_shape
    group, line = n_rows * pair, n_cols // pair
    pixels, channels = mixed.shape
    rank = basis_now.shape[0]
    depth = rank // group
    blocks = pixels // piece

    lanes = wide.shape[3]

    def load_band(block):
        span = slice(block * lanes, (block + 1) * lanes)
        return pltpu.make_async_copy(
            sources[0].at[:, :, span], band.at[:, :, span], band_sem.at[block]
        )

    loads = [
        pltpu.make_async_copy(sources[i], refs[8 + i], load_sem.at[i]) for i in range(1, 7)
    ]
    for block in range(channels // lanes):
        load_band(block).start()
    for load in loads:
        load.start()

    row, col = lax.axis_index("rows"), lax.axis_index("cols")
    cell, along = lax.rem(col, pair), lax.div(col, pair)
    member = row * pair + cell

    def in_group(step):
        other = lax.rem(member + step, group)
        return other, (lax.div(other, pair), along * pair + lax.rem(other, pair))

    def in_line(step):
        return (row, lax.rem(along + step, line) * pair + cell)

    barrier = pltpu.get_barrier_semaphore()
    for step in range(1, group):
        pl.semaphore_signal(barrier, inc=1, device_id=in_group(step)[1], device_id_type=MESH)
    for step in range(1, line):
        pl.semaphore_signal(barrier, inc=1, device_id=in_line(step), device_id_type=MESH)
    greeted = group - 1 + line - 1
    if pair == 2:
        outer = jnp.where(cell == 0, col - 1, col + 1)
        has_outer = jnp.logical_and(outer >= 0, outer < n_cols)

        @pl.when(has_outer)
        def _():
            pl.semaphore_signal(barrier, inc=1, device_id=(row, outer), device_id_type=MESH)

        greeted = greeted + has_outer.astype(jnp.int32)

    filter_strips(
        (n_rows, n_cols), row, col, lambda: pl.semaphore_wait(barrier, greeted),
        load_band, loads, band, column_taps, row_taps, mixed, wide, tall, w_send, w_recv, t_send, t_recv,
    )

    def copy_a(it, step):
        other, device = in_group(step)
        return pltpu.make_async_remote_copy(
            src_ref=part.at[it, other], dst_ref=arrived.at[it, step],
            send_sem=a_send.at[it, step], recv_sem=a_recv.at[it, step],
            device_id=device, device_id_type=MESH,
        )

    def copy_b(it, step):
        return pltpu.make_async_remote_copy(
            src_ref=line_out.at[it], dst_ref=line_in.at[it, step],
            send_sem=b_send.at[it, step], recv_sem=b_recv.at[it, step],
            device_id=in_line(step), device_id_type=MESH,
        )

    def copy_c(it, step, slot):
        return pltpu.make_async_remote_copy(
            src_ref=gathered.at[it, slot], dst_ref=gathered.at[it, slot],
            send_sem=c_send.at[it, step], recv_sem=c_recv.at[it, step],
            device_id=in_group(step)[1], device_id_type=MESH,
        )

    def reduce_all(it, numerator, gram):
        both = jnp.concatenate([numerator, gram, jnp.zeros_like(gram)], axis=1)
        for index in range(group):
            part[it, index] = both[index * depth : (index + 1) * depth]
        for step in range(1, group):
            copy_a(it, step).start()
        total = part[it, member]
        for step in range(1, group):
            copy_a(it, step).wait_recv()
            total = total + arrived[it, step]
        if line > 1:
            line_out[it] = total
            for step in range(1, line):
                copy_b(it, step).start()
            for step in range(1, line):
                copy_b(it, step).wait_recv()
                total = total + line_in[it, step]
        gathered[it, member] = total
        for step in range(1, group):
            copy_c(it, step, member).start()
        for step in range(1, group):
            copy_c(it, step, lax.rem(member + group - step, group)).wait_recv()
        whole = jnp.concatenate([gathered[it, index] for index in range(group)], axis=0)
        return whole[:, :channels], whole[:, channels : channels + rank]

    def squeeze():
        @pl.loop(0, blocks)
        def _(index):
            span = pl.ds(pl.multiple_of(index * piece, piece), piece)
            feature[span, :] = jnp.maximum(dot32(mixed[span, :], w_squeeze[...]), 0.0).astype(
                jnp.bfloat16
            )

    def sums(it):
        basis = basis_now[...]
        basis_low = basis.astype(jnp.bfloat16)
        gram_local = gram_of(jnp.concatenate(split(basis), axis=0))
        for index in range(blocks):
            span = slice(index * piece, (index + 1) * piece)
            top = lax.dot_general(
                basis_low, feature[span, :], NT, preferred_element_type=jnp.float32
            )
            if it == 0:
                weight = jnp.exp(top - jnp.max(top, axis=0, keepdims=True))
                now = weight / jnp.sum(weight, axis=0, keepdims=True)
            else:
                now = coeffs[:, span]
            now = now * top / (product(gram_local, now) + EPS)
            coeffs[:, span] = now
            high, low = split(now)
            halves[:rank, span] = high
            halves[rank:, span] = low
        stacked = halves[...]
        return dot32(stacked[:rank], feature[...]), gram_of(stacked)

    def finish():
        basis = basis_now[...]
        basis_low = basis.astype(jnp.bfloat16)
        gram_local = gram_of(jnp.concatenate(split(basis), axis=0))
        for index in range(blocks):
            span = slice(index * piece, (index + 1) * piece)
            f = feature[span, :]
            top = lax.dot_general(basis_low, f, NT, preferred_element_type=jnp.float32)
            now = coeffs[:, span]
            now = now * top / (product(gram_local, now) + EPS)
            rebuilt = lax.dot_general(
                now.astype(jnp.bfloat16), basis_low, (((0,), (0,)), ((), ())),
                preferred_element_type=jnp.float32,
            ).astype(jnp.bfloat16)
            hammed = jnp.maximum(f.astype(jnp.float32) + dot32(rebuilt, w_ham[...]), 0.0)
            mixed[span, :] = dot32(hammed.astype(jnp.bfloat16), w_align[...]).astype(jnp.bfloat16)
            store(index).start()

    def store(index):
        span = slice(index * piece, (index + 1) * piece)
        return pltpu.make_async_copy(mixed.at[span], out.at[span], out_sem.at[index])

    squeeze()
    for it in range(STEPS):
        numerator, gram = reduce_all(it, *sums(it))
        basis = basis_now[...]
        basis_now[...] = basis * numerator / (product(gram, basis) + EPS)
    finish()
    for it in range(STEPS):
        for step in range(1, group):
            copy_a(it, step).wait_send()
            copy_c(it, step, member).wait_send()
        for step in range(1, line):
            copy_b(it, step).wait_send()
    for index in range(blocks):
        store(index).wait()


def on_device(band_input, column_taps, row_taps, w_squeeze, bases_init, w_ham, w_align):
    n_rows, n_cols = lax.axis_size("rows"), lax.axis_size("cols")
    pair = 2 if n_cols % 2 == 0 else 1
    group, line = n_rows * pair, n_cols // pair
    tile_rows, tile_cols, channels = band_input.shape
    pixels = tile_rows * tile_cols
    margin = column_taps.shape[0] // 2
    rank = bases_init.shape[1]
    depth, width = rank // group, channels + 2 * rank
    piece = 512 if pixels % 512 == 0 else pixels
    lanes = 128
    blocks = channels // lanes
    dma = pltpu.SemaphoreType.DMA
    operands = (band_input, column_taps, row_taps, w_squeeze, bases_init.T, w_ham, w_align)
    head_out = pl.pallas_call(
        functools.partial(factor_kernel, (n_rows, n_cols, pair, piece)),
        out_shape=jax.ShapeDtypeStruct((pixels, channels), jnp.bfloat16),
        in_specs=[pl.BlockSpec(memory_space=pltpu.HBM)] * 7,
        out_specs=pl.BlockSpec(memory_space=pltpu.HBM),
        scratch_shapes=[pltpu.VMEM(x.shape, x.dtype) for x in operands] + [
            pltpu.VMEM((blocks, tile_cols + 2 * margin, tile_rows, lanes), jnp.bfloat16),
            pltpu.VMEM((blocks, tile_rows + 2 * margin, tile_cols, lanes), jnp.bfloat16),
            pltpu.VMEM((pixels, channels), jnp.bfloat16),
            pltpu.VMEM((pixels, channels), jnp.bfloat16),
            pltpu.VMEM((rank, pixels), jnp.float32),
            pltpu.VMEM((2 * rank, pixels), jnp.bfloat16),
            pltpu.VMEM((STEPS, group, depth, width), jnp.float32),
            pltpu.VMEM((STEPS, group, depth, width), jnp.float32),
            pltpu.VMEM((STEPS, depth, width), jnp.float32),
            pltpu.VMEM((STEPS, line, depth, width), jnp.float32),
            pltpu.VMEM((STEPS, group, depth, width), jnp.float32),
            dma((blocks, 2)), dma((blocks, 2)),
            dma((blocks, 2)), dma((blocks, 2)),
            dma((STEPS, group)), dma((STEPS, group)),
            dma((STEPS, line)), dma((STEPS, line)),
            dma((STEPS, group)), dma((STEPS, group)),
            dma((7,)), dma((blocks,)), dma((pixels // piece,)),
        ],
        compiler_params=pltpu.CompilerParams(
            collective_id=0, has_side_effects=True, vmem_limit_bytes=48 * 2**20
        ),
        cost_estimate=pl.CostEstimate(
            flops=6 * pixels * channels * channels, bytes_accessed=8 * pixels * channels,
            transcendentals=0,
        ),
    )(*operands)
    return head_out.reshape(tile_rows, tile_cols, channels)


def solution(mesh):
    in_specs = (P("rows", "cols", None), P(), P(), P(), P(), P(), P())
    out_specs = P("rows", "cols", None)
    return jax.shard_map(
        on_device, mesh=mesh, in_specs=in_specs, out_specs=out_specs, check_vma=False
    )
```

```python
import functools

import jax
import jax.numpy as jnp
from jax import lax
from jax.experimental import pallas as pl
from jax.experimental.pallas import tpu as pltpu
from jax.sharding import PartitionSpec as P

STEPS = 3


EPS = 1e-06

MESH = pl.DeviceIdType.MESH
NT = (((1,), (1,)), ((), ()))


def dot32(a, b):
    return jnp.dot(a, b, preferred_element_type=jnp.float32)


def strip(load, taps, count):
    results = [None] * count
    for index in range(count + len(taps) - 1):
        x = load(index).astype(jnp.float32)
        for target in range(max(0, index - len(taps) + 1), min(count, index + 1)):
            term = taps[index - target] * x
            results[target] = term if results[target] is None else results[target] + term
    return results


def filter_strips(
    counts, row, col, greet, load_band, loads, band, column_taps, row_taps, mixed, wide, tall,
    w_send, w_recv, t_send, t_recv,
):
    n_rows, n_cols = counts
    tile_rows, tile_cols, channels = band.shape
    taps = column_taps.shape[0]
    margin = taps // 2
    lanes = wide.shape[3]
    blocks = channels // lanes
    has = (
        (col > 0, col < n_cols - 1),
        (row > 0, row < n_rows - 1),
    )

    def edge_copy(axis, block, side):
        buffer, length = ((wide, tile_cols), (tall, tile_rows))[axis]
        send, recv = ((w_send, w_recv), (t_send, t_recv))[axis]
        start = margin if side == 0 else length
        target = margin + length if side == 0 else 0
        step = -1 if side == 0 else 1
        device = (row, col + step) if axis == 0 else (row + step, col)
        return pltpu.make_async_remote_copy(
            src_ref=buffer.at[block, pl.ds(start, margin)],
            dst_ref=buffer.at[block, pl.ds(target, margin)],
            send_sem=send.at[block, side], recv_sem=recv.at[block, side],
            device_id=device, device_id_type=MESH,
        )

    def start(axis, block):
        for side in range(2):
            @pl.when(has[axis][side])
            def _():
                edge_copy(axis, block, side).start()

    def wait_send(axis, block):
        for side in range(2):
            @pl.when(has[axis][side])
            def _():
                edge_copy(axis, block, side).wait_send()

    def wait_recv(axis, block):
        for side in range(2):
            @pl.when(has[axis][1 - side])
            def _():
                edge_copy(axis, block, side).wait_recv()

    def clear(axis):
        buffer, length = ((wide, tile_cols), (tall, tile_rows))[axis]
        for side, first in ((0, 0), (1, margin + length)):
            @pl.when(jnp.logical_not(has[axis][side]))
            def _():
                @pl.loop(0, blocks)
                def _(block):
                    buffer[block, first : first + margin] = jnp.zeros(
                        (margin,) + buffer.shape[2:], buffer.dtype
                    )

    def turn(block):
        span = slice(block * lanes, (block + 1) * lanes)

        @pl.loop(0, tile_rows // 16)
        def _(index):
            rows = pl.ds(pl.multiple_of(index * 16, 16), 16)
            x = band[rows, :, span].astype(jnp.float32)
            wide[block, margin : margin + tile_cols, rows, :] = jnp.swapaxes(x, 0, 1).astype(
                jnp.bfloat16
            )

    def across(block):
        span = slice(block * lanes, (block + 1) * lanes)
        halves = tile_cols // 16

        @pl.loop(0, (tile_rows // 16) * halves)
        def _(index):
            h = lax.div(index, halves) * 16
            w = lax.rem(index, halves) * 16
            rows = pl.ds(pl.multiple_of(h, 16), 16)
            factors = [column_taps[k : k + 1, span] for k in range(taps)]
            found = []
            for part in range(2):
                found += strip(
                    lambda i: wide[block, w + part * 8 + i, rows, :], factors, 8
                )
            x = jnp.swapaxes(jnp.stack(found, axis=0), 0, 1).astype(jnp.bfloat16)
            tall[block, pl.ds(margin + h, 16), pl.ds(pl.multiple_of(w, 16), 16), :] = x

    def down(block, first, last):
        span = slice(block * lanes, (block + 1) * lanes)
        halves = tile_cols // 16

        @pl.loop(first * halves, last * halves)
        def _(index):
            h = lax.div(index, halves) * 8
            w = pl.multiple_of(lax.rem(index, halves) * 16, 16)
            factors = [row_taps[k : k + 1, span] for k in range(taps)]
            found = strip(lambda i: tall[block, h + i, pl.ds(w, 16), :], factors, 8)
            for i in range(8):
                x = band[h + i, pl.ds(w, 16), span].astype(jnp.float32) + found[i]
                place = pl.ds(pl.multiple_of((h + i) * tile_cols + w, 16), 16)
                mixed[place, span] = x.astype(jnp.bfloat16)

    load_band(0).wait()
    turn(0)
    greet()
    start(0, 0)
    ahead = min(2, blocks)
    for block in range(1, blocks):
        load_band(block).wait()
        turn(block)
        if block < ahead:
            start(0, block)
    clear(0)
    clear(1)
    for load in loads:
        load.wait()
    strips = tile_rows // 8
    edge = -(-margin // 8)
    for block in range(blocks):
        if block + ahead < blocks:
            wait_send(0, block)
            start(0, block + ahead)
        wait_recv(0, block)
        across(block)
        start(1, block)
        down(block, edge, strips - edge)
        wait_recv(1, block)
        down(block, 0, edge)
        down(block, strips - edge, strips)
    for block in range(blocks):
        if block + ahead >= blocks:
            wait_send(0, block)
        wait_send(1, block)


def split(x):
    high = x.astype(jnp.bfloat16)
    return high, (x - high.astype(jnp.float32)).astype(jnp.bfloat16)


def product(a, b):
    a_high, a_low = split(a)
    b_high, b_low = split(b)
    return dot32(
        jnp.concatenate([a_high, a_low, a_high], axis=1),
        jnp.concatenate([b_high, b_high, b_low], axis=0),
    )


def gram_of(stacked):
    n = stacked.shape[0] // 2
    both = lax.dot_general(stacked, stacked, NT, preferred_element_type=jnp.float32)
    return both[:n, :n] + (both[:n, n:] + both[n:, :n])


def factor_kernel(
    grid_shape, *refs,
):
    sources, out = refs[:7], refs[7]
    band, column_taps, row_taps, w_squeeze, basis_now, w_ham, w_align = refs[8:15]
    (
    wide, tall, mixed, feature, coeffs, halves, part, arrived, line_out, line_in, gathered,
    w_send, w_recv, t_send, t_recv, a_send, a_recv, b_send, b_recv, c_send, c_recv,
    load_sem, band_sem, out_sem,
    ) = refs[15:]
    n_rows, n_cols, pair, piece = grid_shape
    group, line = n_rows * pair, n_cols // pair
    pixels, channels = mixed.shape
    rank = basis_now.shape[0]
    depth = rank // group
    blocks = pixels // piece

    lanes = wide.shape[3]

    def load_band(block):
        span = slice(block * lanes, (block + 1) * lanes)
        return pltpu.make_async_copy(
            sources[0].at[:, :, span], band.at[:, :, span], band_sem.at[block]
        )

    loads = [
        pltpu.make_async_copy(sources[i], refs[8 + i], load_sem.at[i]) for i in range(1, 7)
    ]
    for block in range(channels // lanes):
        load_band(block).start()
    for load in loads:
        load.start()

    row, col = lax.axis_index("rows"), lax.axis_index("cols")
    cell, along = lax.rem(col, pair), lax.div(col, pair)
    member = row * pair + cell

    def in_group(step):
        other = lax.rem(member + step, group)
        return other, (lax.div(other, pair), along * pair + lax.rem(other, pair))

    def in_line(step):
        return (row, lax.rem(along + step, line) * pair + cell)

    barrier = pltpu.get_barrier_semaphore()
    for step in range(1, group):
        pl.semaphore_signal(barrier, inc=1, device_id=in_group(step)[1], device_id_type=MESH)
    for step in range(1, line):
        pl.semaphore_signal(barrier, inc=1, device_id=in_line(step), device_id_type=MESH)
    greeted = group - 1 + line - 1
    if pair == 2:
        outer = jnp.where(cell == 0, col - 1, col + 1)
        has_outer = jnp.logical_and(outer >= 0, outer < n_cols)

        @pl.when(has_outer)
        def _():
            pl.semaphore_signal(barrier, inc=1, device_id=(row, outer), device_id_type=MESH)

        greeted = greeted + has_outer.astype(jnp.int32)

    filter_strips(
        (n_rows, n_cols), row, col, lambda: pl.semaphore_wait(barrier, greeted),
        load_band, loads, band, column_taps, row_taps, mixed, wide, tall, w_send, w_recv, t_send, t_recv,
    )

    def copy_a(it, step):
        other, device = in_group(step)
        return pltpu.make_async_remote_copy(
            src_ref=part.at[it, other], dst_ref=arrived.at[it, step],
            send_sem=a_send.at[it, step], recv_sem=a_recv.at[it, step],
            device_id=device, device_id_type=MESH,
        )

    def copy_b(it, step):
        return pltpu.make_async_remote_copy(
            src_ref=line_out.at[it], dst_ref=line_in.at[it, step],
            send_sem=b_send.at[it, step], recv_sem=b_recv.at[it, step],
            device_id=in_line(step), device_id_type=MESH,
        )

    def copy_c(it, step, slot):
        return pltpu.make_async_remote_copy(
            src_ref=gathered.at[it, slot], dst_ref=gathered.at[it, slot],
            send_sem=c_send.at[it, step], recv_sem=c_recv.at[it, step],
            device_id=in_group(step)[1], device_id_type=MESH,
        )

    def reduce_all(it, numerator, gram):
        both = jnp.concatenate([numerator, gram, jnp.zeros_like(gram)], axis=1)
        for index in range(group):
            part[it, index] = both[index * depth : (index + 1) * depth]
        for step in range(1, group):
            copy_a(it, step).start()
        total = part[it, member]
        for step in range(1, group):
            copy_a(it, step).wait_recv()
            total = total + arrived[it, step]
        if line > 1:
            line_out[it] = total
            for step in range(1, line):
                copy_b(it, step).start()
            for step in range(1, line):
                copy_b(it, step).wait_recv()
                total = total + line_in[it, step]
        gathered[it, member] = total
        for step in range(1, group):
            copy_c(it, step, member).start()
        for step in range(1, group):
            copy_c(it, step, lax.rem(member + group - step, group)).wait_recv()
        whole = jnp.concatenate([gathered[it, index] for index in range(group)], axis=0)
        return whole[:, :channels], whole[:, channels : channels + rank]

    def squeeze():
        @pl.loop(0, blocks)
        def _(index):
            span = pl.ds(pl.multiple_of(index * piece, piece), piece)
            feature[span, :] = jnp.maximum(dot32(mixed[span, :], w_squeeze[...]), 0.0).astype(
                jnp.bfloat16
            )

    def sums(it):
        basis = basis_now[...]
        basis_low = basis.astype(jnp.bfloat16)
        gram_local = gram_of(jnp.concatenate(split(basis), axis=0))
        for index in range(blocks):
            span = slice(index * piece, (index + 1) * piece)
            top = lax.dot_general(
                basis_low, feature[span, :], NT, preferred_element_type=jnp.float32
            )
            if it == 0:
                weight = jnp.exp(top - jnp.max(top, axis=0, keepdims=True))
                now = weight / jnp.sum(weight, axis=0, keepdims=True)
            else:
                now = coeffs[:, span]
            now = now * top / (product(gram_local, now) + EPS)
            coeffs[:, span] = now
            high, low = split(now)
            halves[:rank, span] = high
            halves[rank:, span] = low
        stacked = halves[...]
        return dot32(stacked[:rank], feature[...]), gram_of(stacked)

    def finish():
        basis = basis_now[...]
        basis_low = basis.astype(jnp.bfloat16)
        gram_local = gram_of(jnp.concatenate(split(basis), axis=0))
        for index in range(blocks):
            span = slice(index * piece, (index + 1) * piece)
            f = feature[span, :]
            top = lax.dot_general(basis_low, f, NT, preferred_element_type=jnp.float32)
            now = coeffs[:, span]
            now = now * top / (product(gram_local, now) + EPS)
            rebuilt = lax.dot_general(
                now.astype(jnp.bfloat16), basis_low, (((0,), (0,)), ((), ())),
                preferred_element_type=jnp.float32,
            ).astype(jnp.bfloat16)
            hammed = jnp.maximum(f.astype(jnp.float32) + dot32(rebuilt, w_ham[...]), 0.0)
            mixed[span, :] = dot32(hammed.astype(jnp.bfloat16), w_align[...]).astype(jnp.bfloat16)
            store(index).start()

    def store(index):
        span = slice(index * piece, (index + 1) * piece)
        return pltpu.make_async_copy(mixed.at[span], out.at[span], out_sem.at[index])

    squeeze()
    for it in range(STEPS):
        numerator, gram = reduce_all(it, *sums(it))
        basis = basis_now[...]
        basis_now[...] = basis * numerator / (product(gram, basis) + EPS)
    finish()
    for it in range(STEPS):
        for step in range(1, group):
            copy_a(it, step).wait_send()
            copy_c(it, step, member).wait_send()
        for step in range(1, line):
            copy_b(it, step).wait_send()
    for index in range(blocks):
        store(index).wait()


def on_device(band_input, column_taps, row_taps, w_squeeze, bases_init, w_ham, w_align):
    n_rows, n_cols = lax.axis_size("rows"), lax.axis_size("cols")
    pair = 2 if n_cols % 2 == 0 else 1
    group, line = n_rows * pair, n_cols // pair
    tile_rows, tile_cols, channels = band_input.shape
    pixels = tile_rows * tile_cols
    margin = column_taps.shape[0] // 2
    rank = bases_init.shape[1]
    depth, width = rank // group, channels + 2 * rank
    piece = 512 if pixels % 512 == 0 else pixels
    lanes = 128
    blocks = channels // lanes
    dma = pltpu.SemaphoreType.DMA
    operands = (band_input, column_taps, row_taps, w_squeeze, bases_init.T, w_ham, w_align)
    head_out = pl.pallas_call(
        functools.partial(factor_kernel, (n_rows, n_cols, pair, piece)),
        out_shape=jax.ShapeDtypeStruct((pixels, channels), jnp.bfloat16),
        in_specs=[pl.BlockSpec(memory_space=pltpu.HBM)] * 7,
        out_specs=pl.BlockSpec(memory_space=pltpu.HBM),
        scratch_shapes=[pltpu.VMEM(x.shape, x.dtype) for x in operands] + [
            pltpu.VMEM((blocks, tile_cols + 2 * margin, tile_rows, lanes), jnp.bfloat16),
            pltpu.VMEM((blocks, tile_rows + 2 * margin, tile_cols, lanes), jnp.bfloat16),
            pltpu.VMEM((pixels, channels), jnp.bfloat16),
            pltpu.VMEM((pixels, channels), jnp.bfloat16),
            pltpu.VMEM((rank, pixels), jnp.float32),
            pltpu.VMEM((2 * rank, pixels), jnp.bfloat16),
            pltpu.VMEM((STEPS, group, depth, width), jnp.float32),
            pltpu.VMEM((STEPS, group, depth, width), jnp.float32),
            pltpu.VMEM((STEPS, depth, width), jnp.float32),
            pltpu.VMEM((STEPS, line, depth, width), jnp.float32),
            pltpu.VMEM((STEPS, group, depth, width), jnp.float32),
            dma((blocks, 2)), dma((blocks, 2)),
            dma((blocks, 2)), dma((blocks, 2)),
            dma((STEPS, group)), dma((STEPS, group)),
            dma((STEPS, line)), dma((STEPS, line)),
            dma((STEPS, group)), dma((STEPS, group)),
            dma((7,)), dma((blocks,)), dma((pixels // piece,)),
        ],
        compiler_params=pltpu.CompilerParams(
            collective_id=0, has_side_effects=True, vmem_limit_bytes=63 * 2**20
        ),
        cost_estimate=pl.CostEstimate(
            flops=6 * pixels * channels * channels, bytes_accessed=8 * pixels * channels,
            transcendentals=0,
        ),
    )(*operands)
    return head_out.reshape(tile_rows, tile_cols, channels)


def solution(mesh):
    in_specs = (P("rows", "cols", None), P(), P(), P(), P(), P(), P())
    out_specs = P("rows", "cols", None)
    return jax.shard_map(
        on_device, mesh=mesh, in_specs=in_specs, out_specs=out_specs, check_vma=False
    )
```
